32 devices in a mesh: groups: 2 (over x), seq: 8 (over z, y), mp: 2 (over core).
Axes of the slice: x: 2, y: 2, z: 4, core: 2. Of those that a mesh axis runs over, the one named last changes fastest.
Arguments:
- inputs: bfloat16 [8192, 2560], P(('groups', 'seq')), parts along dimension 0, may hold values from -6 to 6
- zx_weight: bfloat16 [2560, 2, 2560], P('seq', None, 'mp'), may hold values from -0.125 to 0.125
- bc_weight: bfloat16 [2560, 256], P('seq'), may hold values from -0.125 to 0.125
- dt_weight: bfloat16 [2560, 40], P('seq', 'mp'), may hold values from -0.125 to 0.125
- conv_x: float32 [4, 2560], P(None, 'mp'), may hold values from -3 to 3
- conv_x_bias: float32 [2560], P('mp'), may hold values from -3 to 3
- conv_bc: float32 [4, 256], replicated, may hold values from -3 to 3
- conv_bc_bias: float32 [256], replicated, may hold values from -3 to 3
- dt_bias: float32 [40], P('mp'), may hold values from -4 to -3
- decay_log: float32 [40], P('mp'), may hold values from -9 to 0.5
- skip_gain: float32 [40], P('mp'), may hold values from 0.5 to 1.5
- norm_gain: float32 [2560], P('mp'), may hold values from 0.1 to 1.9
- out_weight: bfloat16 [2560, 2560], P('mp', 'seq'), may hold values from -0.125 to 0.125
Outputs:
- mixed: bfloat16 [8192, 2560], P(('groups', 'seq'), 'mp'), parts along dimension 0
The draws below stay inside these ranges and needn't reach their ends.
There are 2 independent parts, one for each index of `groups`. The reference program is written for one: setup_inputs(seed, part) draws one part's arguments, and reference() takes and returns one part's arrays. A program takes and returns all parts, laid end to end along the dimension named above; an argument that names none is the same for every part. Nothing has to cross between parts.
All inputs are finite; a program needn't handle non-finite values.
Results may differ from the reference program's by a relative error of at most 0.0063.
Values may be sent and summed in bfloat16 or wider, within the bound.
A program may use at most 128 MiB of HBM per device.

```python
import jax
import jax.numpy as jnp
from jax import lax

D = 2560
N = 128
CONV = 4
STRETCH = 256
H = 40
DI = 2560
SEQLEN = 4096


def draw_decay_log(key, part):
    pick_key, slow_key, fast_key = jax.random.split(jax.random.fold_in(key, 17), 3)
    slow_share = 0.5
    slow_rates = jax.random.uniform(slow_key, (H,), jnp.float32, -9.0, -6.5)
    fast_rates = jax.random.uniform(fast_key, (H,), jnp.float32, -1.5, 0.5)
    return jnp.where(jax.random.uniform(pick_key, (H,), jnp.float32) < slow_share, slow_rates, fast_rates)


def level_of(own_key, dims, shards, low, largest):
    level = 1.0
    for axis_at, blocks in shards:
        draws = jax.random.uniform(jax.random.fold_in(jax.random.fold_in(own_key, 6), axis_at), (blocks,), jnp.float32, low / len(shards), largest / len(shards))
        level = level * jnp.repeat(jnp.exp(draws), dims[axis_at] // blocks).reshape((-1,) + (1,) * (len(dims) - 1 - axis_at))
    return level


def scatter_about(stream_key, dims, spread, reach, cuts=(), dtype=jnp.bfloat16):
    factor_of = level_of(stream_key, dims, cuts, -0.22, 0.18) if cuts else 1.0
    values = jax.random.normal(stream_key, dims, jnp.float32) * spread * factor_of
    return jnp.minimum(jnp.maximum(values, -reach), reach).astype(dtype)


def setup_inputs(seed: int = 0, part: int = 0) -> dict:
    key_of = jax.random.split(jax.random.key(seed), 14)
    own_keys = jax.random.split(jax.random.fold_in(key_of[13], part), 14)
    return {
        "inputs": scatter_about(own_keys[0], (SEQLEN, D), 1.0, 6.0, ((0, 8),)),
        "zx_weight": scatter_about(key_of[1], (D, 2, DI), D ** -0.5, 0.125, ((0, 8), (2, 2))),
        "bc_weight": scatter_about(key_of[2], (D, 2 * N), D ** -0.5, 0.125, ((0, 8),)),
        "dt_weight": scatter_about(key_of[3], (D, H), D ** -0.5, 0.125, ((0, 8), (1, 2))),
        "conv_x": scatter_about(key_of[4], (CONV, DI), CONV ** -0.5, 3.0, ((1, 2),), jnp.float32),
        "conv_x_bias": scatter_about(key_of[5], (DI,), 0.5, 3.0, ((0, 2),), jnp.float32),
        "conv_bc": scatter_about(key_of[6], (CONV, 2 * N), CONV ** -0.5, 3.0, (), jnp.float32),
        "conv_bc_bias": scatter_about(key_of[7], (2 * N,), 0.5, 3.0, (), jnp.float32),
        "dt_bias": jnp.clip(-4.0 + 1.0 * jax.random.uniform(key_of[8], (H,), jnp.float32) ** level_of(key_of[8], (H,), ((0, 2),), -0.2, 0.2), -4.0, -3.0),
        "decay_log": draw_decay_log(jax.random.fold_in(key_of[13], 71), part),
        "skip_gain": jnp.clip(0.5 + 1.0 * jax.random.uniform(key_of[10], (H,), jnp.float32) ** level_of(key_of[10], (H,), ((0, 2),), -0.2, 0.2), 0.5, 1.5),
        "norm_gain": jnp.clip(1.0 + 0.18 * jax.random.normal(key_of[11], (DI,), jnp.float32), 0.1, 1.9),
        "out_weight": scatter_about(key_of[12], (DI, D), DI ** -0.5, 0.125, ((0, 2), (1, 8))),
    }


HIGHEST = lax.Precision.HIGHEST
NORM_EPS = 1e-05

def conv_silu(padded, kernel, bias_row):
    taps = kernel.shape[0]
    length = padded.shape[0] - taps + 1
    total = jnp.zeros((length, padded.shape[1]), jnp.float32) + bias_row[None, :]
    for tap_index in range(taps):
        total = total + kernel[tap_index][None, :] * padded[tap_index:tap_index + length]
    return jax.nn.silu(total).astype(jnp.bfloat16)

def block_step(state_in, block_inputs):
    values, steps_dt, log_decay, keys_b, queries_c = block_inputs
    span = log_decay.shape[0]
    cumulative = jnp.cumsum(log_decay, axis=0)
    positions = jnp.arange(span)
    causal = positions[:, None] >= positions[None, :]
    across = cumulative.T[:, :, None] - cumulative.T[:, None, :]
    decays = jnp.exp(jnp.where(causal[None, :, :], across, -jnp.inf))
    scores = jnp.dot(queries_c, keys_b.T, preferred_element_type=jnp.float32)
    mixing = (decays * scores[None, :, :] * steps_dt.T[:, None, :]).astype(jnp.bfloat16)
    inner = jnp.einsum('hts,shp->thp', mixing.astype(jnp.float32), values.astype(jnp.float32), precision=HIGHEST)
    queries_wide = queries_c.astype(jnp.float32)
    entering = jnp.einsum('tn,hpn->thp', queries_wide, state_in, precision=HIGHEST) * jnp.exp(cumulative)[:, :, None]
    tail_decay = jnp.exp(cumulative[-1][None, :] - cumulative) * steps_dt
    weighted = (tail_decay[:, :, None] * values.astype(jnp.float32)).astype(jnp.bfloat16)
    state_out = jnp.exp(cumulative[-1])[:, None, None] * state_in + jnp.einsum('shp,sn->hpn', weighted.astype(jnp.float32), keys_b.astype(jnp.float32), precision=HIGHEST)
    return (state_out, inner + entering)

def run_blocks(values, steps_dt, log_decay, keys_b, queries_c):
    length, head_count, head_dim = values.shape
    blocks = length // STRETCH
    state_dim = keys_b.shape[1]

    def to_blocks(array):
        return array.reshape((blocks, STRETCH) + array.shape[1:])
    start_state = jnp.zeros((head_count, head_dim, state_dim), jnp.float32)
    final_state, outputs = lax.scan(block_step, start_state, (to_blocks(values), to_blocks(steps_dt), to_blocks(log_decay), to_blocks(keys_b), to_blocks(queries_c)))
    return (final_state, outputs.reshape(length, head_count, head_dim))

def reference(inputs, zx_weight, bc_weight, dt_weight, conv_x, conv_x_bias, conv_bc, conv_bc_bias, dt_bias, decay_log, skip_gain, norm_gain, out_weight):
    length = inputs.shape[0]
    inner_width = conv_x.shape[1]
    head_count = dt_weight.shape[1]
    head_dim = inner_width // head_count
    state_dim = bc_weight.shape[1] // 2
    taps = conv_x.shape[0]
    projected = jnp.dot(inputs, zx_weight.reshape(zx_weight.shape[0], 2 * inner_width), preferred_element_type=jnp.float32).astype(jnp.bfloat16)
    gate_z = projected[:, :inner_width]
    raw_x = projected[:, inner_width:]
    raw_bc = jnp.dot(inputs, bc_weight, preferred_element_type=jnp.float32).astype(jnp.bfloat16)
    dt_raw = jnp.dot(inputs, dt_weight, preferred_element_type=jnp.float32)
    raw_all = jnp.concatenate([raw_x, raw_bc], axis=1).astype(jnp.float32)
    padded = jnp.concatenate([jnp.zeros((taps - 1, raw_all.shape[1]), jnp.float32), raw_all], axis=0)
    mixed_conv = conv_silu(padded, jnp.concatenate([conv_x, conv_bc], axis=1), jnp.concatenate([conv_x_bias, conv_bc_bias]))
    values = mixed_conv[:, :inner_width].reshape(length, head_count, head_dim)
    keys_b = mixed_conv[:, inner_width:inner_width + state_dim]
    queries_c = mixed_conv[:, inner_width + state_dim:]
    steps_dt = jax.nn.softplus(dt_raw + dt_bias[None, :])
    log_decay = -jnp.exp(decay_log)[None, :] * steps_dt
    final_state, scanned = run_blocks(values, steps_dt, log_decay, keys_b, queries_c)
    output_y = scanned + skip_gain[None, :, None] * values.astype(jnp.float32)
    gated = output_y.reshape(length, inner_width) * jax.nn.silu(gate_z.astype(jnp.float32))
    mean_square = lax.optimization_barrier(jnp.sum(gated * gated, axis=1)) / inner_width
    normed = (gated * lax.rsqrt(mean_square + NORM_EPS)[:, None] * norm_gain[None, :]).astype(jnp.bfloat16)
    return jnp.dot(normed, out_weight, preferred_element_type=jnp.float32).astype(jnp.bfloat16)
```

```python
import jax
import jax.numpy as jnp
from jax import lax
from jax.experimental import pallas as pl
from jax.experimental.pallas import tpu as pltpu
from jax.sharding import PartitionSpec as P

STRETCH = 256
NORM_EPS = 1e-05
HEAD = 64
LANES = 128
BF16 = jnp.bfloat16
F32 = jnp.float32


def turned(block, axis, distance):
    size = lax.axis_size(axis)
    return lax.ppermute(block, axis, [(i, (i + distance) % size) for i in range(size)])


def shifted(block, axis, distance):
    size = lax.axis_size(axis)
    return lax.ppermute(block, axis, [(i, i + distance) for i in range(size - distance)])


def inner_kernel(values_ref, keys_ref, queries_ref, cum_ref, row_ref, y_ref):
    span = values_ref.shape[0]
    heads = cum_ref.shape[1]
    scores = lax.dot_general(
        queries_ref[...], keys_ref[...], (((1,), (1,)), ((), ())), preferred_element_type=F32
    )
    causal = lax.broadcasted_iota(jnp.int32, (span, span), 0) >= lax.broadcasted_iota(
        jnp.int32, (span, span), 1
    )
    for head in range(heads):
        across = cum_ref[:, head : head + 1] + row_ref[head : head + 1, :]
        decays = jnp.exp(jnp.where(causal, across, -jnp.inf))
        mixing = (decays * scores).astype(BF16)
        columns = slice(head * HEAD, (head + 1) * HEAD)
        y_ref[:, columns] = jnp.dot(mixing, values_ref[:, columns], preferred_element_type=F32)


def inner_blocks(values, keys_b, queries_c, cum, row):
    blocks, span, width = values.shape
    heads = cum.shape[2]
    state_dim = keys_b.shape[2]

    def spec(*shape):
        return pl.BlockSpec((None,) + shape, lambda b: (b, 0, 0))

    return pl.pallas_call(
        inner_kernel,
        grid=(blocks,),
        in_specs=[
            spec(span, width),
            spec(span, state_dim),
            spec(span, state_dim),
            spec(span, heads),
            spec(heads, span),
        ],
        out_specs=spec(span, width),
        out_shape=jax.ShapeDtypeStruct((blocks, span, width), F32),
        compiler_params=pltpu.CompilerParams(vmem_limit_bytes=32 * 2**20),
        cost_estimate=pl.CostEstimate(
            flops=2 * blocks * span * span * (width + state_dim),
            bytes_accessed=blocks * span * width * 6,
            transcendentals=blocks * heads * span * span,
        ),
    )(values, keys_b, queries_c, cum, row)


def shards(
    inputs,
    zx_weight,
    bc_weight,
    dt_weight,
    conv_x,
    conv_x_bias,
    conv_bc,
    conv_bc_bias,
    dt_bias,
    decay_log,
    skip_gain,
    norm_gain,
    out_weight,
):
    groups, seqs, cores = (lax.axis_size(a) for a in ("groups", "seq", "mp"))
    group, core = lax.axis_index("groups"), lax.axis_index("mp")
    rows, depth = inputs.shape
    slab = zx_weight.shape[0]
    taps, width_core = conv_x.shape
    heads_core = dt_weight.shape[1]
    width = width_core // groups
    heads = heads_core // groups
    state_dim = bc_weight.shape[1] // 2
    bc_width = 2 * state_dim // cores
    blocks = rows // STRETCH

    def mine(array, axis, size):
        return lax.dynamic_slice_in_dim(array, group * size, size, axis)

    tail = -(-(heads) // LANES) * LANES
    first = jnp.concatenate(
        [
            mine(zx_weight[:, 1, :], 1, width),
            lax.dynamic_slice_in_dim(bc_weight, core * bc_width, bc_width, 1),
            jnp.pad(mine(dt_weight, 1, heads), ((0, 0), (0, tail - heads))),
        ],
        axis=1,
    )
    first_all = lax.all_gather(first, "seq", axis=0, tiled=True)

    part = depth // cores
    own_part = lax.dynamic_slice_in_dim(inputs, core * part, part, 1)
    batches = [inputs]
    for d in range(1, groups):
        arrived = turned(own_part, "groups", d)
        joined = jnp.zeros((rows, depth), BF16)
        joined = lax.dynamic_update_slice_in_dim(joined, arrived, core * part, 1)
        for c in range(1, cores):
            other = turned(arrived, "mp", c)
            joined = lax.dynamic_update_slice_in_dim(
                joined, other, lax.rem(core + cores - c, cores) * part, 1
            )
        batches.append(joined)
    batch = jnp.concatenate(batches, axis=0)

    out_t, first_all = lax.optimization_barrier((mine(out_weight, 0, width).T, first_all))
    out_all = lax.all_gather(out_t, "seq", axis=0, tiled=True)
    z_own, out_all = lax.optimization_barrier((mine(zx_weight[:, 0, :], 1, width), out_all))
    z_all = lax.all_gather(z_own, "seq", axis=0, tiled=True)
    out_pieces = [out_all] + [turned(out_all, "groups", d) for d in range(1, groups)]

    summed = jnp.dot(batch, first_all, preferred_element_type=F32)
    raw_x = summed[:, :width].astype(BF16)
    raw_part = summed[:, width : width + bc_width].astype(BF16)
    dt_raw = summed[:, width + bc_width : width + bc_width + heads]
    raw_bc = jnp.zeros((groups * rows, 2 * state_dim), BF16)
    raw_bc = lax.dynamic_update_slice_in_dim(raw_bc, raw_part, core * bc_width, 1)
    for c in range(1, cores):
        raw_bc = lax.dynamic_update_slice_in_dim(
            raw_bc,
            turned(raw_part, "mp", c),
            lax.rem(core + cores - c, cores) * bc_width,
            1,
        )
    raw_all = jnp.concatenate([raw_x, raw_bc], axis=1).reshape(groups, rows, width + 2 * state_dim)
    rim_rows = shifted(raw_all[:, rows - (taps - 1) :], "seq", 1)
    padded = jnp.concatenate([rim_rows, raw_all], axis=1)
    kernel = jnp.concatenate([mine(conv_x, 1, width), conv_bc], axis=1)
    total = jnp.concatenate([mine(conv_x_bias, 0, width), conv_bc_bias])[None, None, :]
    for tap in range(taps):
        total = total + kernel[tap][None, None, :] * padded[:, tap : tap + rows].astype(F32)
    mixed_conv = jax.nn.silu(total).astype(BF16)

    batch_blocks = groups * blocks
    mixed_conv = mixed_conv.reshape(batch_blocks, STRETCH, width + 2 * state_dim)
    values = mixed_conv[:, :, :width]
    keys_b = mixed_conv[:, :, width : width + state_dim]
    queries_c = mixed_conv[:, :, width + state_dim :]
    steps_dt = jax.nn.softplus(dt_raw + mine(dt_bias, 0, heads)[None, :])
    log_decay = -jnp.exp(mine(decay_log, 0, heads))[None, :] * steps_dt
    steps_dt = steps_dt.reshape(batch_blocks, STRETCH, heads)
    cum = jnp.cumsum(log_decay.reshape(batch_blocks, STRETCH, heads), axis=1)
    cum_last = cum[:, -1, :]

    def wide(array):
        return jnp.repeat(array, HEAD, axis=-1)

    tail_decay = jnp.exp(cum_last[:, None, :] - cum) * steps_dt
    weighted = (wide(tail_decay) * values.astype(F32)).astype(BF16)
    block_states = jnp.einsum(
        "bsw,bsn->bwn", weighted, keys_b, preferred_element_type=F32
    ).reshape(groups, blocks, width, state_dim)
    block_decay = jnp.exp(cum_last).reshape(groups, blocks, heads)
    held = [jnp.zeros((groups, width, state_dim), F32)]
    passed = [jnp.ones((groups, heads), F32)]
    for b in range(blocks):
        held.append(wide(block_decay[:, b])[:, :, None] * held[-1] + block_states[:, b])
        passed.append(passed[-1] * block_decay[:, b])

    def packed(state, decay):
        high = decay.astype(BF16)
        low = (decay - high.astype(F32)).astype(BF16)
        extra = jnp.stack([high, low], axis=1)
        extra = jnp.pad(extra, ((0, 0), (0, 14), (0, state_dim - heads)))
        return jnp.concatenate([state.astype(BF16), extra], axis=1)

    def unpacked(message):
        decay = message[:, width, :heads].astype(F32) + message[:, width + 1, :heads].astype(F32)
        return message[:, :width].astype(F32), decay

    message = packed(held[-1], passed[-1])
    state, decay = unpacked(shifted(message, "seq", 1))
    if seqs > 2:
        far_state, far_decay = unpacked(shifted(message, "seq", 2))
        state = state + wide(decay)[:, :, None] * far_state
        decay = decay * far_decay
    reach = 2
    while reach < seqs - 1:
        far_state, far_decay = unpacked(shifted(packed(state, decay), "seq", reach))
        state = state + wide(decay)[:, :, None] * far_state
        decay = decay * far_decay
        reach *= 2

    inner = inner_blocks(
        values, keys_b, queries_c, cum, (jnp.log(steps_dt) - cum).transpose(0, 2, 1)
    )

    gate_z = jnp.dot(batch, z_all, preferred_element_type=F32).astype(BF16)

    state_in = jnp.stack(
        [held[b] + wide(passed[b])[:, :, None] * state for b in range(blocks)], axis=1
    ).reshape(batch_blocks, width, state_dim)
    entering = jnp.einsum(
        "bsn,bwn->bsw", queries_c, state_in.astype(BF16), preferred_element_type=F32
    )
    skip = wide(mine(skip_gain, 0, heads))[None, None, :]
    output_y = inner + wide(jnp.exp(cum)) * entering + skip * values.astype(F32)
    gated = output_y.reshape(groups, rows, width) * jax.nn.silu(
        gate_z.astype(F32).reshape(groups, rows, width)
    )
    squares = jnp.sum(gated * gated, axis=2)
    scaled = (gated * mine(norm_gain, 0, width)[None, None, :]).astype(BF16)

    partial = jnp.zeros((rows, seqs * out_weight.shape[1]), F32)
    square = jnp.zeros((rows,), F32)
    for d in range(groups):
        at = (-d) % groups
        piece, square_piece = scaled[at], squares[at]
        if d:
            piece, square_piece = turned(piece, "groups", d), turned(square_piece, "groups", d)
        partial = partial + lax.dot_general(
            piece, out_pieces[d], (((1,), (1,)), ((), ())), preferred_element_type=F32
        )
        square = square + square_piece
    columns = partial.shape[1] // cores
    mixed = lax.dynamic_slice_in_dim(partial, core * columns, columns, 1)
    total_square = square
    for c in range(1, cores):
        theirs = lax.dynamic_slice_in_dim(
            partial, lax.rem(core + c, cores) * columns, columns, 1
        ).astype(BF16)
        mixed = mixed + turned(theirs, "mp", c).astype(F32)
        total_square = total_square + turned(square, "mp", c)
    mean_square = total_square / (width_core * cores)
    return (mixed * lax.rsqrt(mean_square + NORM_EPS)[:, None]).astype(BF16)


def solution(mesh):
    return jax.shard_map(
        shards,
        mesh=mesh,
        in_specs=(
            P(("groups", "seq"), None),
            P("seq", None, "mp"),
            P("seq", None),
            P("seq", "mp"),
            P(None, "mp"),
            P("mp"),
            P(),
            P(),
            P("mp"),
            P("mp"),
            P("mp"),
            P("mp"),
            P("mp", "seq"),
        ),
        out_specs=P(("groups", "seq"), "mp"),
        check_vma=False,
    )
```

```python
import functools

import jax
import jax.numpy as jnp
from jax import lax
from jax.experimental import pallas as pl
from jax.experimental.pallas import tpu as pltpu
from jax.sharding import PartitionSpec as P

STRETCH = 256
NORM_EPS = 1e-05
HEAD = 64
LANES = 128
BF16 = jnp.bfloat16
F32 = jnp.float32


def turned(block, axis, distance):
    size = lax.axis_size(axis)
    return lax.ppermute(block, axis, [(i, (i + distance) % size) for i in range(size)])


def shifted(block, axis, distance):
    size = lax.axis_size(axis)
    return lax.ppermute(block, axis, [(i, i + distance) for i in range(size - distance)])


def inner_kernel(values_ref, keys_ref, queries_ref, cum_ref, row_ref, y_ref):
    span = values_ref.shape[0]
    heads = cum_ref.shape[1]
    scores = lax.dot_general(
        queries_ref[...], keys_ref[...], (((1,), (1,)), ((), ())), preferred_element_type=F32
    )
    causal = lax.broadcasted_iota(jnp.int32, (span, span), 0) >= lax.broadcasted_iota(
        jnp.int32, (span, span), 1
    )
    for head in range(heads):
        across = cum_ref[:, head : head + 1] + row_ref[head : head + 1, :]
        decays = jnp.exp(jnp.where(causal, across, -jnp.inf))
        mixing = (decays * scores).astype(BF16)
        columns = slice(head * HEAD, (head + 1) * HEAD)
        y_ref[:, columns] = jnp.dot(mixing, values_ref[:, columns], preferred_element_type=F32)


def inner_blocks(values, keys_b, queries_c, cum, row):
    blocks, span, width = values.shape
    heads = cum.shape[2]
    state_dim = keys_b.shape[2]

    def spec(*shape):
        return pl.BlockSpec((None,) + shape, lambda b: (b, 0, 0))

    return pl.pallas_call(
        inner_kernel,
        grid=(blocks,),
        in_specs=[
            spec(span, width),
            spec(span, state_dim),
            spec(span, state_dim),
            spec(span, heads),
            spec(heads, span),
        ],
        out_specs=spec(span, width),
        out_shape=jax.ShapeDtypeStruct((blocks, span, width), F32),
        compiler_params=pltpu.CompilerParams(vmem_limit_bytes=32 * 2**20),
        cost_estimate=pl.CostEstimate(
            flops=2 * blocks * span * span * (width + state_dim),
            bytes_accessed=blocks * span * width * 6,
            transcendentals=blocks * heads * span * span,
        ),
    )(values, keys_b, queries_c, cum, row)

MESH_ID = pl.DeviceIdType.MESH


def gather_kernel(sizes, first_ref, out_ref, z_ref, x_ref, first_all, out_all, z_all, arrived, *sems):
    groups, seqs, cores = sizes
    ring_send, ring_recv, side_send, side_recv, x_send, x_recv, core_send, core_recv, own_sem = sems
    group, seq, core = (lax.axis_index(a) for a in ("groups", "seq", "mp"))
    odd = lax.rem(seq, 2)
    half_at = lax.div(seq, 2)
    place = (1 - odd) * half_at + odd * (seqs - 1 - half_at)

    def seq_at(position):
        position = lax.rem(position + 2 * seqs, seqs)
        back = lax.div(position, seqs // 2)
        return (1 - back) * 2 * position + back * (2 * (seqs - 1 - position) + 1)

    def group_at(d):
        return lax.rem(group + d, groups)

    def core_at(c):
        return lax.rem(core + c, cores)

    barrier = pltpu.get_barrier_semaphore()
    near = [{"seq": seq_at(place + 1)}, {"seq": seq_at(place - 1)}]
    near += [{"groups": group_at(d)} for d in range(1, groups)]
    near += [{"mp": core_at(c)} for c in range(1, cores)]
    for other in near:
        pl.semaphore_signal(barrier, inc=1, device_id=other, device_id_type=MESH_ID)
    pl.semaphore_wait(barrier, len(near))

    part = x_ref.shape[1] // cores
    columns = pl.ds(pl.multiple_of(core * part, 128), part)
    x_copies = []
    for d in range(1, groups):
        x_copies.append(
            pltpu.make_async_remote_copy(
                src_ref=x_ref.at[:, columns],
                dst_ref=arrived.at[d - 1, :, columns],
                send_sem=x_send.at[d - 1],
                recv_sem=x_recv.at[d - 1],
                device_id={"groups": group_at(d)},
                device_id_type=MESH_ID,
            )
        )
    for copy in x_copies:
        copy.start()

    owns = [first_ref, out_ref.at[0], z_ref]
    alls = [first_all, out_all.at[0], z_all]
    locals_ = [(first_ref, first_all.at[seq]), (z_ref, z_all.at[seq])]
    locals_ += [(out_ref.at[d], out_all.at[d, seq]) for d in range(groups)]
    own_copies = [
        pltpu.make_async_copy(source, target, own_sem.at[i])
        for i, (source, target) in enumerate(locals_)
    ]

    slab = first_ref.shape[0]
    cut = (slab // 2 + 15) // 16 * 16
    spans = [pl.ds(0, cut), pl.ds(cut, slab - cut)]
    steps = seqs // 2
    counts = [[steps, seqs - 1 - steps], [seqs - 1 - steps, steps]]
    everything, sides, core_copies = [], [], []

    def ring_copy(k, half, way, step):
        owner = seq_at(place - step if way == 0 else place + step)
        source = owns[k] if step == 0 else alls[k].at[owner]
        return pltpu.make_async_remote_copy(
            src_ref=source.at[spans[half]],
            dst_ref=alls[k].at[owner, spans[half]],
            send_sem=ring_send.at[k, half, way, step],
            recv_sem=ring_recv.at[k, half, way, step],
            device_id={"seq": seq_at(place + 1 if way == 0 else place - 1)},
            device_id_type=MESH_ID,
        )

    def received(k, half, way, step, copy):
        copy.wait_recv()
        if k != 1:
            return
        owner = seq_at(place - 1 - step if way == 0 else place + 1 + step)
        for d in range(1, groups):
            side = pltpu.make_async_remote_copy(
                src_ref=out_all.at[0, owner, spans[half]],
                dst_ref=out_all.at[d, owner, spans[half]],
                send_sem=side_send.at[d - 1, half, way, step],
                recv_sem=side_recv.at[d - 1, half, way, step],
                device_id={"groups": group_at(d)},
                device_id_type=MESH_ID,
            )
            side.start()
            sides.append(side)

    late = {}
    for k in range(3):
        for step in range(steps):
            for half in range(2):
                for way in range(2):
                    if step >= counts[half][way]:
                        continue
                    if step:
                        received(k, half, way, step - 1, late.pop((k, half, way)))
                    copy = ring_copy(k, half, way, step)
                    copy.start()
                    everything.append(copy)
                    late[(k, half, way)] = copy
            if step == 0 and k == 0:
                for copy in own_copies:
                    copy.start()
            if step == 0 and k:
                for half in range(2):
                    for way in range(2):
                        received(k - 1, half, way, counts[half][way] - 1, late.pop((k - 1, half, way)))
        if k == 0:
            for d, copy in enumerate(x_copies):
                copy.wait_recv()
                for c in range(1, cores):
                    on = pltpu.make_async_remote_copy(
                        src_ref=arrived.at[d, :, columns],
                        dst_ref=arrived.at[d, :, columns],
                        send_sem=core_send.at[d, c - 1],
                        recv_sem=core_recv.at[d, c - 1],
                        device_id={"mp": core_at(c)},
                        device_id_type=MESH_ID,
                    )
                    on.start()
                    core_copies.append(on)
    for half in range(2):
        for way in range(2):
            received(2, half, way, counts[half][way] - 1, late.pop((2, half, way)))
    for copy in sides + core_copies:
        copy.wait_recv()
    for copy in everything + sides + core_copies + x_copies:
        copy.wait_send()
    for copy in own_copies:
        copy.wait()


def gathered(sizes, first, out_t, z_own, inputs):
    groups, seqs, cores = sizes
    steps = seqs // 2
    anywhere = pl.BlockSpec(memory_space=pl.ANY)
    dma = pltpu.SemaphoreType.DMA

    def like(lead, array):
        return jax.ShapeDtypeStruct(lead + array.shape, array.dtype)

    others, peers = max(groups - 1, 1), max(cores - 1, 1)
    return pl.pallas_call(
        functools.partial(gather_kernel, sizes),
        in_specs=[anywhere] * 4,
        out_specs=[anywhere] * 4,
        out_shape=[
            like((seqs,), first),
            like((groups, seqs), out_t[0]),
            like((seqs,), z_own),
            like((others,), inputs),
        ],
        scratch_shapes=[
            dma((3, 2, 2, steps)),
            dma((3, 2, 2, steps)),
            dma((others, 2, 2, steps)),
            dma((others, 2, 2, steps)),
            dma((others,)),
            dma((others,)),
            dma((others, peers)),
            dma((others, peers)),
            dma((2 + groups,)),
        ],
        compiler_params=pltpu.CompilerParams(collective_id=0, has_side_effects=True),
    )(first, out_t, z_own, inputs)


def shards(
    inputs,
    zx_weight,
    bc_weight,
    dt_weight,
    conv_x,
    conv_x_bias,
    conv_bc,
    conv_bc_bias,
    dt_bias,
    decay_log,
    skip_gain,
    norm_gain,
    out_weight,
):
    groups, seqs, cores = (lax.axis_size(a) for a in ("groups", "seq", "mp"))
    group, core = lax.axis_index("groups"), lax.axis_index("mp")
    rows, depth = inputs.shape
    slab = zx_weight.shape[0]
    taps, width_core = conv_x.shape
    heads_core = dt_weight.shape[1]
    width = width_core // groups
    heads = heads_core // groups
    state_dim = bc_weight.shape[1] // 2
    bc_width = 2 * state_dim // cores
    blocks = rows // STRETCH

    def mine(array, axis, size):
        return lax.dynamic_slice_in_dim(array, group * size, size, axis)

    tail = -(-(heads) // LANES) * LANES
    first = jnp.concatenate(
        [
            mine(zx_weight[:, 1, :], 1, width),
            lax.dynamic_slice_in_dim(bc_weight, core * bc_width, bc_width, 1),
            jnp.pad(mine(dt_weight, 1, heads), ((0, 0), (0, tail - heads))),
        ],
        axis=1,
    )
    out_t = jnp.stack(
        [
            lax.dynamic_slice_in_dim(
                out_weight, lax.rem(group + groups - d, groups) * width, width, 0
            ).T
            for d in range(groups)
        ]
    )
    first_all, out_pieces, z_all, arrived = gathered(
        (groups, seqs, cores), first, out_t, mine(zx_weight[:, 0, :], 1, width), inputs
    )
    first_all = first_all.reshape(seqs * slab, first.shape[1])
    z_all = z_all.reshape(seqs * slab, width)
    out_pieces = [out_pieces[d].reshape(-1, width) for d in range(groups)]
    batch = jnp.concatenate([inputs[None], arrived], axis=0).reshape(groups * rows, depth)

    summed = jnp.dot(batch, first_all, preferred_element_type=F32)
    raw_x = summed[:, :width].astype(BF16)
    raw_part = summed[:, width : width + bc_width].astype(BF16)
    dt_raw = summed[:, width + bc_width : width + bc_width + heads]
    raw_bc = jnp.zeros((groups * rows, 2 * state_dim), BF16)
    raw_bc = lax.dynamic_update_slice_in_dim(raw_bc, raw_part, core * bc_width, 1)
    for c in range(1, cores):
        raw_bc = lax.dynamic_update_slice_in_dim(
            raw_bc,
            turned(raw_part, "mp", c),
            lax.rem(core + cores - c, cores) * bc_width,
            1,
        )
    raw_all = jnp.concatenate([raw_x, raw_bc], axis=1).reshape(groups, rows, width + 2 * state_dim)
    rim_rows = shifted(raw_all[:, rows - (taps - 1) :], "seq", 1)
    padded = jnp.concatenate([rim_rows, raw_all], axis=1)
    kernel = jnp.concatenate([mine(conv_x, 1, width), conv_bc], axis=1)
    total = jnp.concatenate([mine(conv_x_bias, 0, width), conv_bc_bias])[None, None, :]
    for tap in range(taps):
        total = total + kernel[tap][None, None, :] * padded[:, tap : tap + rows].astype(F32)
    mixed_conv = jax.nn.silu(total).astype(BF16)

    batch_blocks = groups * blocks
    mixed_conv = mixed_conv.reshape(batch_blocks, STRETCH, width + 2 * state_dim)
    values = mixed_conv[:, :, :width]
    keys_b = mixed_conv[:, :, width : width + state_dim]
    queries_c = mixed_conv[:, :, width + state_dim :]
    steps_dt = jax.nn.softplus(dt_raw + mine(dt_bias, 0, heads)[None, :])
    log_decay = -jnp.exp(mine(decay_log, 0, heads))[None, :] * steps_dt
    steps_dt = steps_dt.reshape(batch_blocks, STRETCH, heads)
    cum = jnp.cumsum(log_decay.reshape(batch_blocks, STRETCH, heads), axis=1)
    cum_last = cum[:, -1, :]

    def wide(array):
        return jnp.repeat(array, HEAD, axis=-1)

    tail_decay = jnp.exp(cum_last[:, None, :] - cum) * steps_dt
    weighted = (wide(tail_decay) * values.astype(F32)).astype(BF16)
    block_states = jnp.einsum(
        "bsw,bsn->bwn", weighted, keys_b, preferred_element_type=F32
    ).reshape(groups, blocks, width, state_dim)
    block_decay = jnp.exp(cum_last).reshape(groups, blocks, heads)
    held = [jnp.zeros((groups, width, state_dim), F32)]
    passed = [jnp.ones((groups, heads), F32)]
    for b in range(blocks):
        held.append(wide(block_decay[:, b])[:, :, None] * held[-1] + block_states[:, b])
        passed.append(passed[-1] * block_decay[:, b])

    def packed(state, decay):
        high = decay.astype(BF16)
        low = (decay - high.astype(F32)).astype(BF16)
        extra = jnp.stack([high, low], axis=1)
        extra = jnp.pad(extra, ((0, 0), (0, 14), (0, state_dim - heads)))
        return jnp.concatenate([state.astype(BF16), extra], axis=1)

    def unpacked(message):
        decay = message[:, width, :heads].astype(F32) + message[:, width + 1, :heads].astype(F32)
        return message[:, :width].astype(F32), decay

    message = packed(held[-1], passed[-1])
    state, decay = unpacked(shifted(message, "seq", 1))
    if seqs > 2:
        far_state, far_decay = unpacked(shifted(message, "seq", 2))
        state = state + wide(decay)[:, :, None] * far_state
        decay = decay * far_decay
    reach = 2
    while reach < seqs - 1:
        far_state, far_decay = unpacked(shifted(packed(state, decay), "seq", reach))
        state = state + wide(decay)[:, :, None] * far_state
        decay = decay * far_decay
        reach *= 2

    inner = inner_blocks(
        values, keys_b, queries_c, cum, (jnp.log(steps_dt) - cum).transpose(0, 2, 1)
    )

    gate_z = jnp.dot(batch, z_all, preferred_element_type=F32).astype(BF16)

    state_in = jnp.stack(
        [held[b] + wide(passed[b])[:, :, None] * state for b in range(blocks)], axis=1
    ).reshape(batch_blocks, width, state_dim)
    entering = jnp.einsum(
        "bsn,bwn->bsw", queries_c, state_in.astype(BF16), preferred_element_type=F32
    )
    skip = wide(mine(skip_gain, 0, heads))[None, None, :]
    output_y = inner + wide(jnp.exp(cum)) * entering + skip * values.astype(F32)
    gated = output_y.reshape(groups, rows, width) * jax.nn.silu(
        gate_z.astype(F32).reshape(groups, rows, width)
    )
    squares = jnp.sum(gated * gated, axis=2)
    scaled = (gated * mine(norm_gain, 0, width)[None, None, :]).astype(BF16)

    partial = jnp.zeros((rows, seqs * out_weight.shape[1]), F32)
    square = jnp.zeros((rows,), F32)
    for d in range(groups):
        at = (-d) % groups
        piece, square_piece = scaled[at], squares[at]
        if d:
            piece, square_piece = turned(piece, "groups", d), turned(square_piece, "groups", d)
        partial = partial + lax.dot_general(
            piece, out_pieces[d], (((1,), (1,)), ((), ())), preferred_element_type=F32
        )
        square = square + square_piece
    columns = partial.shape[1] // cores
    mixed = lax.dynamic_slice_in_dim(partial, core * columns, columns, 1)
    total_square = square
    for c in range(1, cores):
        theirs = lax.dynamic_slice_in_dim(
            partial, lax.rem(core + c, cores) * columns, columns, 1
        ).astype(BF16)
        mixed = mixed + turned(theirs, "mp", c).astype(F32)
        total_square = total_square + turned(square, "mp", c)
    mean_square = total_square / (width_core * cores)
    return (mixed * lax.rsqrt(mean_square + NORM_EPS)[:, None]).astype(BF16)


def solution(mesh):
    return jax.shard_map(
        shards,
        mesh=mesh,
        in_specs=(
            P(("groups", "seq"), None),
            P("seq", None, "mp"),
            P("seq", None),
            P("seq", "mp"),
            P(None, "mp"),
            P("mp"),
            P(),
            P(),
            P("mp"),
            P("mp"),
            P("mp"),
            P("mp"),
            P("mp", "seq"),
        ),
        out_specs=P(("groups", "seq"), "mp"),
        check_vma=False,
    )
```

```python
import functools

import jax
import jax.numpy as jnp
from jax import lax
from jax.experimental import pallas as pl
from jax.experimental.pallas import tpu as pltpu
from jax.sharding import PartitionSpec as P

STRETCH = 256
NORM_EPS = 1e-05
HEAD = 64
LANES = 128
BF16 = jnp.bfloat16
F32 = jnp.float32


def turned(block, axis, distance):
    size = lax.axis_size(axis)
    return lax.ppermute(block, axis, [(i, (i + distance) % size) for i in range(size)])


def shifted(block, axis, distance):
    size = lax.axis_size(axis)
    return lax.ppermute(block, axis, [(i, i + distance) for i in range(size - distance)])


def inner_kernel(values_ref, keys_ref, queries_ref, cum_ref, row_ref, y_ref):
    span = values_ref.shape[0]
    heads = cum_ref.shape[1]
    scores = lax.dot_general(
        queries_ref[...], keys_ref[...], (((1,), (1,)), ((), ())), preferred_element_type=F32
    )
    causal = lax.broadcasted_iota(jnp.int32, (span, span), 0) >= lax.broadcasted_iota(
        jnp.int32, (span, span), 1
    )
    for head in range(heads):
        across = cum_ref[:, head : head + 1] + row_ref[head : head + 1, :]
        decays = jnp.exp(jnp.where(causal, across, -jnp.inf))
        mixing = (decays * scores).astype(BF16)
        columns = slice(head * HEAD, (head + 1) * HEAD)
        y_ref[:, columns] = jnp.dot(mixing, values_ref[:, columns], preferred_element_type=F32)


def inner_blocks(values, keys_b, queries_c, cum, row):
    blocks, span, width = values.shape
    heads = cum.shape[2]
    state_dim = keys_b.shape[2]

    def spec(*shape):
        return pl.BlockSpec((None,) + shape, lambda b: (b, 0, 0))

    return pl.pallas_call(
        inner_kernel,
        grid=(blocks,),
        in_specs=[
            spec(span, width),
            spec(span, state_dim),
            spec(span, state_dim),
            spec(span, heads),
            spec(heads, span),
        ],
        out_specs=spec(span, width),
        out_shape=jax.ShapeDtypeStruct((blocks, span, width), F32),
        compiler_params=pltpu.CompilerParams(vmem_limit_bytes=32 * 2**20),
        cost_estimate=pl.CostEstimate(
            flops=2 * blocks * span * span * (width + state_dim),
            bytes_accessed=blocks * span * width * 6,
            transcendentals=blocks * heads * span * span,
        ),
    )(values, keys_b, queries_c, cum, row)

MESH_ID = pl.DeviceIdType.MESH


def gather_kernel(sizes, first_ref, out_ref, x_ref, first_all, out_all, arrived, *sems):
    groups, seqs, cores = sizes
    ring_send, ring_recv, side_send, side_recv, x_send, x_recv, core_send, core_recv, own_sem = sems
    group, seq, core = (lax.axis_index(a) for a in ("groups", "seq", "mp"))
    odd = lax.rem(seq, 2)
    half_at = lax.div(seq, 2)
    place = (1 - odd) * half_at + odd * (seqs - 1 - half_at)

    def seq_at(position):
        position = lax.rem(position + 2 * seqs, seqs)
        back = lax.div(position, seqs // 2)
        return (1 - back) * 2 * position + back * (2 * (seqs - 1 - position) + 1)

    def group_at(d):
        return lax.rem(group + d, groups)

    def core_at(c):
        return lax.rem(core + c, cores)

    barrier = pltpu.get_barrier_semaphore()
    near = [{"seq": seq_at(place + 1)}, {"seq": seq_at(place - 1)}]
    near += [{"groups": group_at(d)} for d in range(1, groups)]
    near += [{"mp": core_at(c)} for c in range(1, cores)]
    for other in near:
        pl.semaphore_signal(barrier, inc=1, device_id=other, device_id_type=MESH_ID)
    pl.semaphore_wait(barrier, len(near))

    part = x_ref.shape[1] // cores
    columns = pl.ds(pl.multiple_of(core * part, 128), part)
    x_copies = []
    for d in range(1, groups):
        x_copies.append(
            pltpu.make_async_remote_copy(
                src_ref=x_ref.at[:, columns],
                dst_ref=arrived.at[d - 1, :, columns],
                send_sem=x_send.at[d - 1],
                recv_sem=x_recv.at[d - 1],
                device_id={"groups": group_at(d)},
                device_id_type=MESH_ID,
            )
        )
    for copy in x_copies:
        copy.start()

    owns = [first_ref, out_ref.at[0]]
    alls = [first_all, out_all.at[0]]
    locals_ = [(first_ref, first_all.at[seq])]
    locals_ += [(out_ref.at[d], out_all.at[d, seq]) for d in range(groups)]
    own_copies = [
        pltpu.make_async_copy(source, target, own_sem.at[i])
        for i, (source, target) in enumerate(locals_)
    ]

    slab = first_ref.shape[0]
    cut = (slab // 2 + 15) // 16 * 16
    spans = [pl.ds(0, cut), pl.ds(cut, slab - cut)]
    steps = seqs // 2
    counts = [[steps, seqs - 1 - steps], [seqs - 1 - steps, steps]]
    everything, sides, core_copies = [], [], []

    def ring_copy(k, half, way, step):
        owner = seq_at(place - step if way == 0 else place + step)
        source = owns[k] if step == 0 else alls[k].at[owner]
        return pltpu.make_async_remote_copy(
            src_ref=source.at[spans[half]],
            dst_ref=alls[k].at[owner, spans[half]],
            send_sem=ring_send.at[k, half, way, step],
            recv_sem=ring_recv.at[k, half, way, step],
            device_id={"seq": seq_at(place + 1 if way == 0 else place - 1)},
            device_id_type=MESH_ID,
        )

    def received(k, half, way, step, copy):
        copy.wait_recv()
        if k != 1:
            return
        owner = seq_at(place - 1 - step if way == 0 else place + 1 + step)
        for d in range(1, groups):
            side = pltpu.make_async_remote_copy(
                src_ref=out_all.at[0, owner, spans[half]],
                dst_ref=out_all.at[d, owner, spans[half]],
                send_sem=side_send.at[d - 1, half, way, step],
                recv_sem=side_recv.at[d - 1, half, way, step],
                device_id={"groups": group_at(d)},
                device_id_type=MESH_ID,
            )
            side.start()
            sides.append(side)

    late = {}
    for k in range(2):
        for step in range(steps):
            for half in range(2):
                for way in range(2):
                    if step >= counts[half][way]:
                        continue
                    if step:
                        received(k, half, way, step - 1, late.pop((k, half, way)))
                    copy = ring_copy(k, half, way, step)
                    copy.start()
                    everything.append(copy)
                    late[(k, half, way)] = copy
            if step == 0 and k == 0:
                for copy in own_copies:
                    copy.start()
            if step == 0 and k:
                for half in range(2):
                    for way in range(2):
                        received(k - 1, half, way, counts[half][way] - 1, late.pop((k - 1, half, way)))
        if k == 0:
            for d, copy in enumerate(x_copies):
                copy.wait_recv()
                for c in range(1, cores):
                    on = pltpu.make_async_remote_copy(
                        src_ref=arrived.at[d, :, columns],
                        dst_ref=arrived.at[d, :, columns],
                        send_sem=core_send.at[d, c - 1],
                        recv_sem=core_recv.at[d, c - 1],
                        device_id={"mp": core_at(c)},
                        device_id_type=MESH_ID,
                    )
                    on.start()
                    core_copies.append(on)
    for half in range(2):
        for way in range(2):
            received(1, half, way, counts[half][way] - 1, late.pop((1, half, way)))
    for copy in sides + core_copies:
        copy.wait_recv()
    for copy in everything + sides + core_copies + x_copies:
        copy.wait_send()
    for copy in own_copies:
        copy.wait()


def gathered(sizes, first, out_t, inputs):
    groups, seqs, cores = sizes
    steps = seqs // 2
    anywhere = pl.BlockSpec(memory_space=pl.ANY)
    dma = pltpu.SemaphoreType.DMA

    def like(lead, array):
        return jax.ShapeDtypeStruct(lead + array.shape, array.dtype)

    others, peers = max(groups - 1, 1), max(cores - 1, 1)
    return pl.pallas_call(
        functools.partial(gather_kernel, sizes),
        in_specs=[anywhere] * 3,
        out_specs=[anywhere] * 3,
        out_shape=[
            like((seqs,), first),
            like((groups, seqs), out_t[0]),
            like((others,), inputs),
        ],
        scratch_shapes=[
            dma((2, 2, 2, steps)),
            dma((2, 2, 2, steps)),
            dma((others, 2, 2, steps)),
            dma((others, 2, 2, steps)),
            dma((others,)),
            dma((others,)),
            dma((others, peers)),
            dma((others, peers)),
            dma((1 + groups,)),
        ],
        compiler_params=pltpu.CompilerParams(collective_id=0, has_side_effects=True),
        cost_estimate=pl.CostEstimate(flops=0, bytes_accessed=200 * 2**20, transcendentals=0),
    )(first, out_t, inputs)


def shards(
    inputs,
    zx_weight,
    bc_weight,
    dt_weight,
    conv_x,
    conv_x_bias,
    conv_bc,
    conv_bc_bias,
    dt_bias,
    decay_log,
    skip_gain,
    norm_gain,
    out_weight,
):
    groups, seqs, cores = (lax.axis_size(a) for a in ("groups", "seq", "mp"))
    group, core = lax.axis_index("groups"), lax.axis_index("mp")
    rows, depth = inputs.shape
    slab = zx_weight.shape[0]
    taps, width_core = conv_x.shape
    heads_core = dt_weight.shape[1]
    width = width_core // groups
    heads = heads_core // groups
    state_dim = bc_weight.shape[1] // 2
    bc_width = 2 * state_dim // cores
    blocks = rows // STRETCH

    def mine(array, axis, size):
        return lax.dynamic_slice_in_dim(array, group * size, size, axis)

    tail = -(-(heads) // LANES) * LANES
    first = jnp.concatenate(
        [
            mine(zx_weight[:, 1, :], 1, width),
            lax.dynamic_slice_in_dim(bc_weight, core * bc_width, bc_width, 1),
            jnp.pad(mine(dt_weight, 1, heads), ((0, 0), (0, tail - heads))),
        ],
        axis=1,
    )
    out_t = jnp.stack(
        [
            lax.dynamic_slice_in_dim(
                out_weight, lax.rem(group + groups - d, groups) * width, width, 0
            ).T
            for d in range(groups)
        ]
    )
    z_all = lax.all_gather(mine(zx_weight[:, 0, :], 1, width), "seq", axis=0, tiled=True)
    first_all, out_pieces, arrived = gathered((groups, seqs, cores), first, out_t, inputs)
    first_all = first_all.reshape(seqs * slab, first.shape[1])
    out_pieces = [out_pieces[d].reshape(-1, width) for d in range(groups)]
    batch = jnp.concatenate([inputs[None], arrived], axis=0).reshape(groups * rows, depth)

    summed = jnp.dot(batch, first_all, preferred_element_type=F32)
    raw_x = summed[:, :width].astype(BF16)
    raw_part = summed[:, width : width + bc_width].astype(BF16)
    dt_raw = summed[:, width + bc_width : width + bc_width + heads]
    raw_bc = jnp.zeros((groups * rows, 2 * state_dim), BF16)
    raw_bc = lax.dynamic_update_slice_in_dim(raw_bc, raw_part, core * bc_width, 1)
    for c in range(1, cores):
        raw_bc = lax.dynamic_update_slice_in_dim(
            raw_bc,
            turned(raw_part, "mp", c),
            lax.rem(core + cores - c, cores) * bc_width,
            1,
        )
    raw_all = jnp.concatenate([raw_x, raw_bc], axis=1).reshape(groups, rows, width + 2 * state_dim)
    rim_rows = shifted(raw_all[:, rows - (taps - 1) :], "seq", 1)
    padded = jnp.concatenate([rim_rows, raw_all], axis=1)
    kernel = jnp.concatenate([mine(conv_x, 1, width), conv_bc], axis=1)
    total = jnp.concatenate([mine(conv_x_bias, 0, width), conv_bc_bias])[None, None, :]
    for tap in range(taps):
        total = total + kernel[tap][None, None, :] * padded[:, tap : tap + rows].astype(F32)
    mixed_conv = jax.nn.silu(total).astype(BF16)

    batch_blocks = groups * blocks
    mixed_conv = mixed_conv.reshape(batch_blocks, STRETCH, width + 2 * state_dim)
    values = mixed_conv[:, :, :width]
    keys_b = mixed_conv[:, :, width : width + state_dim]
    queries_c = mixed_conv[:, :, width + state_dim :]
    steps_dt = jax.nn.softplus(dt_raw + mine(dt_bias, 0, heads)[None, :])
    log_decay = -jnp.exp(mine(decay_log, 0, heads))[None, :] * steps_dt
    steps_dt = steps_dt.reshape(batch_blocks, STRETCH, heads)
    cum = jnp.cumsum(log_decay.reshape(batch_blocks, STRETCH, heads), axis=1)
    cum_last = cum[:, -1, :]

    def wide(array):
        return jnp.repeat(array, HEAD, axis=-1)

    tail_decay = jnp.exp(cum_last[:, None, :] - cum) * steps_dt
    weighted = (wide(tail_decay) * values.astype(F32)).astype(BF16)
    block_states = jnp.einsum(
        "bsw,bsn->bwn", weighted, keys_b, preferred_element_type=F32
    ).reshape(groups, blocks, width, state_dim)
    block_decay = jnp.exp(cum_last).reshape(groups, blocks, heads)
    held = [jnp.zeros((groups, width, state_dim), F32)]
    passed = [jnp.ones((groups, heads), F32)]
    for b in range(blocks):
        held.append(wide(block_decay[:, b])[:, :, None] * held[-1] + block_states[:, b])
        passed.append(passed[-1] * block_decay[:, b])

    def packed(state, decay):
        high = decay.astype(BF16)
        low = (decay - high.astype(F32)).astype(BF16)
        extra = jnp.stack([high, low], axis=1)
        extra = jnp.pad(extra, ((0, 0), (0, 14), (0, state_dim - heads)))
        return jnp.concatenate([state.astype(BF16), extra], axis=1)

    def unpacked(message):
        decay = message[:, width, :heads].astype(F32) + message[:, width + 1, :heads].astype(F32)
        return message[:, :width].astype(F32), decay

    inner = inner_blocks(
        values, keys_b, queries_c, cum, (jnp.log(steps_dt) - cum).transpose(0, 2, 1)
    )
    gate_z = jnp.dot(batch, z_all, preferred_element_type=F32).astype(BF16)
    message = packed(held[-1], passed[-1])
    near, far = shifted(message, "seq", 1), shifted(message, "seq", 2)
    near, far, inner = lax.optimization_barrier((near, far, inner))
    state, decay = unpacked(near)
    if seqs > 2:
        far_state, far_decay = unpacked(far)
        state = state + wide(decay)[:, :, None] * far_state
        decay = decay * far_decay
    reach = 2
    while reach < seqs - 1:
        far = shifted(packed(state, decay), "seq", reach)
        if reach == 2:
            far, gate_z = lax.optimization_barrier((far, gate_z))
        far_state, far_decay = unpacked(far)
        state = state + wide(decay)[:, :, None] * far_state
        decay = decay * far_decay
        reach *= 2

    state_in = jnp.stack(
        [held[b] + wide(passed[b])[:, :, None] * state for b in range(blocks)], axis=1
    ).reshape(batch_blocks, width, state_dim)
    entering = jnp.einsum(
        "bsn,bwn->bsw", queries_c, state_in.astype(BF16), preferred_element_type=F32
    )
    skip = wide(mine(skip_gain, 0, heads))[None, None, :]
    output_y = inner + wide(jnp.exp(cum)) * entering + skip * values.astype(F32)
    gated = output_y.reshape(groups, rows, width) * jax.nn.silu(
        gate_z.astype(F32).reshape(groups, rows, width)
    )
    squares = jnp.sum(gated * gated, axis=2)
    scaled = (gated * mine(norm_gain, 0, width)[None, None, :]).astype(BF16)

    partial = jnp.zeros((rows, seqs * out_weight.shape[1]), F32)
    square = jnp.zeros((rows,), F32)
    for d in range(groups):
        at = (-d) % groups
        piece, square_piece = scaled[at], squares[at]
        if d:
            piece, square_piece = turned(piece, "groups", d), turned(square_piece, "groups", d)
        partial = partial + lax.dot_general(
            piece, out_pieces[d], (((1,), (1,)), ((), ())), preferred_element_type=F32
        )
        square = square + square_piece
    columns = partial.shape[1] // cores
    mixed = lax.dynamic_slice_in_dim(partial, core * columns, columns, 1)
    total_square = square
    for c in range(1, cores):
        theirs = lax.dynamic_slice_in_dim(
            partial, lax.rem(core + c, cores) * columns, columns, 1
        ).astype(BF16)
        mixed = mixed + turned(theirs, "mp", c).astype(F32)
        total_square = total_square + turned(square, "mp", c)
    mean_square = total_square / (width_core * cores)
    return (mixed * lax.rsqrt(mean_square + NORM_EPS)[:, None]).astype(BF16)


def solution(mesh):
    return jax.shard_map(
        shards,
        mesh=mesh,
        in_specs=(
            P(("groups", "seq"), None),
            P("seq", None, "mp"),
            P("seq", None),
            P("seq", "mp"),
            P(None, "mp"),
            P("mp"),
            P(),
            P(),
            P("mp"),
            P("mp"),
            P("mp"),
            P("mp"),
            P("mp", "seq"),
        ),
        out_specs=P(("groups", "seq"), "mp"),
        check_vma=False,
    )
```

```python
import functools

import jax
import jax.numpy as jnp
from jax import lax
from jax.experimental import pallas as pl
from jax.experimental.pallas import tpu as pltpu
from jax.sharding import PartitionSpec as P

STRETCH = 256
NORM_EPS = 1e-05
HEAD = 64
LANES = 128
BF16 = jnp.bfloat16
F32 = jnp.float32


def turned(block, axis, distance):
    size = lax.axis_size(axis)
    return lax.ppermute(block, axis, [(i, (i + distance) % size) for i in range(size)])


def shifted(block, axis, distance):
    size = lax.axis_size(axis)
    return lax.ppermute(block, axis, [(i, i + distance) for i in range(size - distance)])


def inner_kernel(values_ref, keys_ref, queries_ref, cum_ref, row_ref, y_ref):
    span = values_ref.shape[0]
    heads = cum_ref.shape[1]
    scores = lax.dot_general(
        queries_ref[...], keys_ref[...], (((1,), (1,)), ((), ())), preferred_element_type=F32
    )
    causal = lax.broadcasted_iota(jnp.int32, (span, span), 0) >= lax.broadcasted_iota(
        jnp.int32, (span, span), 1
    )
    for head in range(heads):
        across = cum_ref[:, head : head + 1] + row_ref[head : head + 1, :]
        decays = jnp.exp(jnp.where(causal, across, -jnp.inf))
        mixing = (decays * scores).astype(BF16)
        columns = slice(head * HEAD, (head + 1) * HEAD)
        y_ref[:, columns] = jnp.dot(mixing, values_ref[:, columns], preferred_element_type=F32)


def inner_blocks(values, keys_b, queries_c, cum, row):
    blocks, span, width = values.shape
    heads = cum.shape[2]
    state_dim = keys_b.shape[2]

    def spec(*shape):
        return pl.BlockSpec((None,) + shape, lambda b: (b, 0, 0))

    return pl.pallas_call(
        inner_kernel,
        grid=(blocks,),
        in_specs=[
            spec(span, width),
            spec(span, state_dim),
            spec(span, state_dim),
            spec(span, heads),
            spec(heads, span),
        ],
        out_specs=spec(span, width),
        out_shape=jax.ShapeDtypeStruct((blocks, span, width), F32),
        compiler_params=pltpu.CompilerParams(vmem_limit_bytes=32 * 2**20),
        cost_estimate=pl.CostEstimate(
            flops=2 * blocks * span * span * (width + state_dim),
            bytes_accessed=blocks * span * width * 6,
            transcendentals=blocks * heads * span * span,
        ),
    )(values, keys_b, queries_c, cum, row)

MESH_ID = pl.DeviceIdType.MESH


def gather_kernel(sizes, first_ref, out_ref, x_ref, first_all, out_all, arrived, *sems):
    groups, seqs, cores = sizes
    ring_send, ring_recv, side_send, side_recv, x_send, x_recv, core_send, core_recv, own_sem = sems
    group, seq, core = (lax.axis_index(a) for a in ("groups", "seq", "mp"))
    odd = lax.rem(seq, 2)
    half_at = lax.div(seq, 2)
    place = (1 - odd) * half_at + odd * (seqs - 1 - half_at)

    def seq_at(position):
        position = lax.rem(position + 2 * seqs, seqs)
        back = lax.div(position, seqs // 2)
        return (1 - back) * 2 * position + back * (2 * (seqs - 1 - position) + 1)

    def group_at(d):
        return lax.rem(group + d, groups)

    def core_at(c):
        return lax.rem(core + c, cores)

    barrier = pltpu.get_barrier_semaphore()
    near = [{"seq": seq_at(place + 1)}, {"seq": seq_at(place - 1)}]
    near += [{"groups": group_at(d)} for d in range(1, groups)]
    near += [{"mp": core_at(c)} for c in range(1, cores)]
    for other in near:
        pl.semaphore_signal(barrier, inc=1, device_id=other, device_id_type=MESH_ID)
    pl.semaphore_wait(barrier, len(near))

    part = x_ref.shape[1] // cores
    columns = pl.ds(pl.multiple_of(core * part, 128), part)
    x_copies = []
    for d in range(1, groups):
        x_copies.append(
            pltpu.make_async_remote_copy(
                src_ref=x_ref.at[:, columns],
                dst_ref=arrived.at[d - 1, :, columns],
                send_sem=x_send.at[d - 1],
                recv_sem=x_recv.at[d - 1],
                device_id={"groups": group_at(d)},
                device_id_type=MESH_ID,
            )
        )
    for copy in x_copies:
        copy.start()

    owns = [first_ref, out_ref.at[0]]
    alls = [first_all, out_all.at[0]]
    locals_ = [(first_ref, first_all.at[seq])]
    locals_ += [(out_ref.at[d], out_all.at[d, seq]) for d in range(groups)]
    own_copies = [
        pltpu.make_async_copy(source, target, own_sem.at[i])
        for i, (source, target) in enumerate(locals_)
    ]

    slab = first_ref.shape[0]
    cut = (slab // 2 + 15) // 16 * 16
    spans = [pl.ds(0, cut), pl.ds(cut, slab - cut)]
    steps = seqs // 2
    counts = [[steps, seqs - 1 - steps], [seqs - 1 - steps, steps]]
    everything, sides, core_copies = [], [], []

    def ring_copy(k, half, way, step):
        owner = seq_at(place - step if way == 0 else place + step)
        source = owns[k] if step == 0 else alls[k].at[owner]
        return pltpu.make_async_remote_copy(
            src_ref=source.at[spans[half]],
            dst_ref=alls[k].at[owner, spans[half]],
            send_sem=ring_send.at[k, half, way, step],
            recv_sem=ring_recv.at[k, half, way, step],
            device_id={"seq": seq_at(place + 1 if way == 0 else place - 1)},
            device_id_type=MESH_ID,
        )

    def received(k, half, way, step, copy):
        copy.wait_recv()
        if k != 1:
            return
        owner = seq_at(place - 1 - step if way == 0 else place + 1 + step)
        for d in range(1, groups):
            side = pltpu.make_async_remote_copy(
                src_ref=out_all.at[0, owner, spans[half]],
                dst_ref=out_all.at[d, owner, spans[half]],
                send_sem=side_send.at[d - 1, half, way, step],
                recv_sem=side_recv.at[d - 1, half, way, step],
                device_id={"groups": group_at(d)},
                device_id_type=MESH_ID,
            )
            side.start()
            sides.append(side)

    late = {}
    for k in range(2):
        for step in range(steps):
            for half in range(2):
                for way in range(2):
                    if step >= counts[half][way]:
                        continue
                    if step:
                        received(k, half, way, step - 1, late.pop((k, half, way)))
                    copy = ring_copy(k, half, way, step)
                    copy.start()
                    everything.append(copy)
                    late[(k, half, way)] = copy
            if step == 0 and k == 0:
                for copy in own_copies:
                    copy.start()
            if step == 0 and k:
                for half in range(2):
                    for way in range(2):
                        received(k - 1, half, way, counts[half][way] - 1, late.pop((k - 1, half, way)))
        if k == 0:
            for d, copy in enumerate(x_copies):
                copy.wait_recv()
                for c in range(1, cores):
                    on = pltpu.make_async_remote_copy(
                        src_ref=arrived.at[d, :, columns],
                        dst_ref=arrived.at[d, :, columns],
                        send_sem=core_send.at[d, c - 1],
                        recv_sem=core_recv.at[d, c - 1],
                        device_id={"mp": core_at(c)},
                        device_id_type=MESH_ID,
                    )
                    on.start()
                    core_copies.append(on)
    for half in range(2):
        for way in range(2):
            received(1, half, way, counts[half][way] - 1, late.pop((1, half, way)))
    for copy in sides + core_copies:
        copy.wait_recv()
    for copy in everything + sides + core_copies + x_copies:
        copy.wait_send()
    for copy in own_copies:
        copy.wait()


def gathered(sizes, first, out_t, inputs):
    groups, seqs, cores = sizes
    steps = seqs // 2
    anywhere = pl.BlockSpec(memory_space=pl.ANY)
    dma = pltpu.SemaphoreType.DMA

    def like(lead, array):
        return jax.ShapeDtypeStruct(lead + array.shape, array.dtype)

    others, peers = max(groups - 1, 1), max(cores - 1, 1)
    return pl.pallas_call(
        functools.partial(gather_kernel, sizes),
        in_specs=[anywhere] * 3,
        out_specs=[anywhere] * 3,
        out_shape=[
            like((seqs,), first),
            like((groups, seqs), out_t[0]),
            like((others,), inputs),
        ],
        scratch_shapes=[
            dma((2, 2, 2, steps)),
            dma((2, 2, 2, steps)),
            dma((others, 2, 2, steps)),
            dma((others, 2, 2, steps)),
            dma((others,)),
            dma((others,)),
            dma((others, peers)),
            dma((others, peers)),
            dma((1 + groups,)),
        ],
        compiler_params=pltpu.CompilerParams(collective_id=0, has_side_effects=True),
        cost_estimate=pl.CostEstimate(flops=0, bytes_accessed=200 * 2**20, transcendentals=0),
    )(first, out_t, inputs)


def shards(
    inputs,
    zx_weight,
    bc_weight,
    dt_weight,
    conv_x,
    conv_x_bias,
    conv_bc,
    conv_bc_bias,
    dt_bias,
    decay_log,
    skip_gain,
    norm_gain,
    out_weight,
):
    groups, seqs, cores = (lax.axis_size(a) for a in ("groups", "seq", "mp"))
    group, core = lax.axis_index("groups"), lax.axis_index("mp")
    rows, depth = inputs.shape
    slab = zx_weight.shape[0]
    taps, width_core = conv_x.shape
    heads_core = dt_weight.shape[1]
    width = width_core // groups
    heads = heads_core // groups
    state_dim = bc_weight.shape[1] // 2
    bc_width = 2 * state_dim // cores
    blocks = rows // STRETCH

    def mine(array, axis, size):
        return lax.dynamic_slice_in_dim(array, group * size, size, axis)

    tail = -(-(heads) // LANES) * LANES
    first = jnp.concatenate(
        [
            mine(zx_weight[:, 1, :], 1, width),
            lax.dynamic_slice_in_dim(bc_weight, core * bc_width, bc_width, 1),
            jnp.pad(mine(dt_weight, 1, heads), ((0, 0), (0, tail - heads))),
        ],
        axis=1,
    )
    out_t = jnp.stack(
        [
            lax.dynamic_slice_in_dim(
                out_weight, lax.rem(group + groups - d, groups) * width, width, 0
            ).T
            for d in range(groups)
        ]
    )
    first_all, out_pieces, arrived = gathered((groups, seqs, cores), first, out_t, inputs)
    z_own, first_all = lax.optimization_barrier((mine(zx_weight[:, 0, :], 1, width), first_all))
    z_all = lax.all_gather(z_own, "seq", axis=0, tiled=True)
    first_all = first_all.reshape(seqs * slab, first.shape[1])
    out_pieces = [out_pieces[d].reshape(-1, width) for d in range(groups)]
    batch = jnp.concatenate([inputs[None], arrived], axis=0).reshape(groups * rows, depth)

    summed = jnp.dot(batch, first_all, preferred_element_type=F32)
    raw_x = summed[:, :width].astype(BF16)
    raw_part = summed[:, width : width + bc_width].astype(BF16)
    dt_raw = summed[:, width + bc_width : width + bc_width + heads]
    raw_bc = jnp.zeros((groups * rows, 2 * state_dim), BF16)
    raw_bc = lax.dynamic_update_slice_in_dim(raw_bc, raw_part, core * bc_width, 1)
    for c in range(1, cores):
        raw_bc = lax.dynamic_update_slice_in_dim(
            raw_bc,
            turned(raw_part, "mp", c),
            lax.rem(core + cores - c, cores) * bc_width,
            1,
        )
    raw_all = jnp.concatenate([raw_x, raw_bc], axis=1).reshape(groups, rows, width + 2 * state_dim)
    rim_rows = shifted(raw_all[:, rows - (taps - 1) :], "seq", 1)
    padded = jnp.concatenate([rim_rows, raw_all], axis=1)
    kernel = jnp.concatenate([mine(conv_x, 1, width), conv_bc], axis=1)
    total = jnp.concatenate([mine(conv_x_bias, 0, width), conv_bc_bias])[None, None, :]
    for tap in range(taps):
        total = total + kernel[tap][None, None, :] * padded[:, tap : tap + rows].astype(F32)
    mixed_conv = jax.nn.silu(total).astype(BF16)

    batch_blocks = groups * blocks
    mixed_conv = mixed_conv.reshape(batch_blocks, STRETCH, width + 2 * state_dim)
    values = mixed_conv[:, :, :width]
    keys_b = mixed_conv[:, :, width : width + state_dim]
    queries_c = mixed_conv[:, :, width + state_dim :]
    steps_dt = jax.nn.softplus(dt_raw + mine(dt_bias, 0, heads)[None, :])
    log_decay = -jnp.exp(mine(decay_log, 0, heads))[None, :] * steps_dt
    steps_dt = steps_dt.reshape(batch_blocks, STRETCH, heads)
    cum = jnp.cumsum(log_decay.reshape(batch_blocks, STRETCH, heads), axis=1)
    cum_last = cum[:, -1, :]

    def wide(array):
        return jnp.repeat(array, HEAD, axis=-1)

    tail_decay = jnp.exp(cum_last[:, None, :] - cum) * steps_dt
    weighted = (wide(tail_decay) * values.astype(F32)).astype(BF16)
    block_states = jnp.einsum(
        "bsw,bsn->bwn", weighted, keys_b, preferred_element_type=F32
    ).reshape(groups, blocks, width, state_dim)
    block_decay = jnp.exp(cum_last).reshape(groups, blocks, heads)
    held = [jnp.zeros((groups, width, state_dim), F32)]
    passed = [jnp.ones((groups, heads), F32)]
    for b in range(blocks):
        held.append(wide(block_decay[:, b])[:, :, None] * held[-1] + block_states[:, b])
        passed.append(passed[-1] * block_decay[:, b])

    def packed(state, decay):
        high = decay.astype(BF16)
        low = (decay - high.astype(F32)).astype(BF16)
        extra = jnp.stack([high, low], axis=1)
        extra = jnp.pad(extra, ((0, 0), (0, 14), (0, state_dim - heads)))
        return jnp.concatenate([state.astype(BF16), extra], axis=1)

    def unpacked(message):
        decay = message[:, width, :heads].astype(F32) + message[:, width + 1, :heads].astype(F32)
        return message[:, :width].astype(F32), decay

    inner = inner_blocks(
        values, keys_b, queries_c, cum, (jnp.log(steps_dt) - cum).transpose(0, 2, 1)
    )
    gate_z = jnp.dot(batch, z_all, preferred_element_type=F32).astype(BF16)
    message = packed(held[-1], passed[-1])
    near, far = shifted(message, "seq", 1), shifted(message, "seq", 2)
    near, far, inner = lax.optimization_barrier((near, far, inner))
    state, decay = unpacked(near)
    if seqs > 2:
        far_state, far_decay = unpacked(far)
        state = state + wide(decay)[:, :, None] * far_state
        decay = decay * far_decay
    reach = 2
    while reach < seqs - 1:
        far = shifted(packed(state, decay), "seq", reach)
        if 2 * reach >= seqs - 1:
            far, gate_z = lax.optimization_barrier((far, gate_z))
        far_state, far_decay = unpacked(far)
        state = state + wide(decay)[:, :, None] * far_state
        decay = decay * far_decay
        reach *= 2

    state_in = jnp.stack(
        [held[b] + wide(passed[b])[:, :, None] * state for b in range(blocks)], axis=1
    ).reshape(batch_blocks, width, state_dim)
    entering = jnp.einsum(
        "bsn,bwn->bsw", queries_c, state_in.astype(BF16), preferred_element_type=F32
    )
    skip = wide(mine(skip_gain, 0, heads))[None, None, :]
    output_y = inner + wide(jnp.exp(cum)) * entering + skip * values.astype(F32)
    gated = output_y.reshape(groups, rows, width) * jax.nn.silu(
        gate_z.astype(F32).reshape(groups, rows, width)
    )
    squares = jnp.sum(gated * gated, axis=2)
    scaled = (gated * mine(norm_gain, 0, width)[None, None, :]).astype(BF16)

    partial = jnp.zeros((rows, seqs * out_weight.shape[1]), F32)
    square = jnp.zeros((rows,), F32)
    for d in range(groups):
        at = (-d) % groups
        piece, square_piece = scaled[at], squares[at]
        if d:
            piece, square_piece = turned(piece, "groups", d), turned(square_piece, "groups", d)
        partial = partial + lax.dot_general(
            piece, out_pieces[d], (((1,), (1,)), ((), ())), preferred_element_type=F32
        )
        square = square + square_piece
    columns = partial.shape[1] // cores
    mixed = lax.dynamic_slice_in_dim(partial, core * columns, columns, 1)
    total_square = square
    for c in range(1, cores):
        theirs = lax.dynamic_slice_in_dim(
            partial, lax.rem(core + c, cores) * columns, columns, 1
        ).astype(BF16)
        mixed = mixed + turned(theirs, "mp", c).astype(F32)
        total_square = total_square + turned(square, "mp", c)
    mean_square = total_square / (width_core * cores)
    return (mixed * lax.rsqrt(mean_square + NORM_EPS)[:, None]).astype(BF16)


def solution(mesh):
    return jax.shard_map(
        shards,
        mesh=mesh,
        in_specs=(
            P(("groups", "seq"), None),
            P("seq", None, "mp"),
            P("seq", None),
            P("seq", "mp"),
            P(None, "mp"),
            P("mp"),
            P(),
            P(),
            P("mp"),
            P("mp"),
            P("mp"),
            P("mp"),
            P("mp", "seq"),
        ),
        out_specs=P(("groups", "seq"), "mp"),
        check_vma=False,
    )
```
